32 devices in a mesh: groups: 4 (over y, core), shards: 2 (over x), tensor: 4 (over z).
Axes of the slice: x: 2, y: 2, z: 4, core: 2. Of those that a mesh axis runs over, the one named last changes fastest.
Arguments:
- global_layer: float32 [3, 2816, 1024], P(None, 'tensor', 'shards'), may hold values from -6 to 6
- local_layer: bfloat16 [4, 3, 2816, 1024], P('groups', None, 'tensor', 'shards'), may hold values from -6 to 6
- layer_momentum: float32 [3, 2816, 1024], P(None, 'tensor', 'shards'), may hold values from -6 to 6
- global_embed: float32 [32000, 1024], P('shards', 'tensor'), may hold values from -6 to 6
- local_embed: bfloat16 [4, 32000, 1024], P('groups', 'shards', 'tensor'), may hold values from -6 to 6
- embed_momentum: float32 [32000, 1024], P('shards', 'tensor'), may hold values from -6 to 6
- projection: float32 [1024, 64], P('tensor'), may hold values from -0.1875 to 0.1875
Outputs:
- new_layer: float32 [3, 2816, 1024], P(None, 'tensor', 'shards')
- new_layer_momentum: float32 [3, 2816, 1024], P(None, 'tensor', 'shards')
- new_embed: float32 [32000, 1024], P('shards', 'tensor')
- new_embed_momentum: float32 [32000, 1024], P('shards', 'tensor')
The draws below stay inside these ranges and needn't reach their ends.
All inputs are finite; a program needn't handle non-finite values.
Results may differ from the reference program's by a relative error of at most 0.0003.
Values sent between devices are 32-bit elements; how exact they have to be, the bound alone decides.
No kernel may reach another device: no remote copies, remote signals or barrier semaphores. Data moves between devices by JAX's collectives and lax.ppermute only.
A program may use at most 192 MiB of HBM per device.

```python
import jax
import jax.numpy as jnp
from jax import lax

D = 1024
FF = 2816
VOCAB = 32000
RANK = 64
LAYERS = 1
GROUPS = 4
N_GROUPS = 4


def shard_levels(key, shape, cuts, smallest, high):
    gain = 1.0
    for axis_at, parts in cuts:
        steps = jax.random.uniform(jax.random.fold_in(jax.random.fold_in(key, 6), axis_at), (parts,), jnp.float32, smallest / len(cuts), high / len(cuts))
        gain = gain * jnp.repeat(jnp.exp(steps), shape[axis_at] // parts).reshape((-1,) + (1,) * (len(shape) - 1 - axis_at))
    return gain


def noise(rng, shape, spread, bound, cuts=(), dtype=jnp.bfloat16):
    entries = spread * jax.random.normal(rng, shape, jnp.float32)
    if cuts:
        entries = entries * shard_levels(rng, shape, cuts, -0.22, 0.18)
    return jnp.clip(entries, -bound, bound).astype(dtype)


def setup_inputs(seed: int = 0) -> dict:
    key_list = jax.random.split(jax.random.key(seed), 8)
    global_layer = noise(key_list[0], (3 * LAYERS, FF, D), 1.0, 6.0, ((1, 4), (2, 2)), jnp.float32)
    local_layer = noise(key_list[1], (GROUPS, 3 * LAYERS, FF, D), 1.0, 6.0, ((0, 4), (2, 4), (3, 2)))
    layer_momentum = noise(key_list[2], (3 * LAYERS, FF, D), 0.5, 6.0, ((1, 4), (2, 2)), jnp.float32)
    global_embed = noise(key_list[3], (VOCAB, D), 1.0, 6.0, ((0, 2), (1, 4)), jnp.float32)
    local_embed = noise(key_list[4], (GROUPS, VOCAB, D), 1.0, 6.0, ((0, 4), (1, 2), (2, 4)))
    embed_momentum = noise(key_list[5], (VOCAB, D), 0.5, 6.0, ((0, 2), (1, 4)), jnp.float32)
    projection = noise(key_list[6], (D, RANK), D ** -0.5, 0.1875, ((0, 4),), jnp.float32)
    return {"global_layer": global_layer, "local_layer": local_layer, "layer_momentum": layer_momentum, "global_embed": global_embed, "local_embed": local_embed, "embed_momentum": embed_momentum, "projection": projection}


momentum_rate = 0.9
outer_rate = 0.7


def reference(global_layer, local_layer, layer_momentum, global_embed, local_embed, embed_momentum, projection):
    layer_total = jnp.zeros(global_layer.shape, jnp.float32)
    for group in range(N_GROUPS):
        layer_total = layer_total + (global_layer - local_layer[group].astype(jnp.float32))
    layer_delta = layer_total / N_GROUPS
    new_layer_momentum = momentum_rate * layer_momentum + layer_delta
    new_layer = global_layer - outer_rate * (layer_delta + momentum_rate * new_layer_momentum)
    projected = jnp.zeros((global_embed.shape[0], projection.shape[1]), jnp.float32)
    for group in range(N_GROUPS):
        difference = global_embed - local_embed[group].astype(jnp.float32)
        projected = projected + jnp.dot(difference, projection, precision=lax.Precision.HIGHEST, preferred_element_type=jnp.float32)
    projected = projected / N_GROUPS
    embed_delta = jnp.dot(projected, projection.T, precision=lax.Precision.HIGHEST, preferred_element_type=jnp.float32)
    new_embed_momentum = momentum_rate * embed_momentum + embed_delta
    new_embed = global_embed - outer_rate * (embed_delta + momentum_rate * new_embed_momentum)
    return new_layer, new_layer_momentum, new_embed, new_embed_momentum
```

```python
import functools

import jax
import jax.numpy as jnp
import numpy as np
from jax import lax
from jax.experimental import pallas as pl
from jax.experimental.pallas import tpu as pltpu
from jax.sharding import PartitionSpec as P

momentum_rate = 0.9
outer_rate = 0.7
GRAIN = 16
UNIT = 176
COST = pl.CostEstimate(flops=0, bytes_accessed=0, transcendentals=0)
PARAMS = pltpu.CompilerParams(vmem_limit_bytes=53 * 1024 * 1024)


def nesterov(weights, momentum, delta):
    moved = momentum_rate * momentum + delta
    return (weights - outer_rate * (delta + momentum_rate * moved), moved)


def halves(value):
    high = value.astype(jnp.bfloat16)
    return high, (value - high.astype(jnp.float32)).astype(jnp.bfloat16)


def dot(a, b):
    return jnp.dot(a, b, preferred_element_type=jnp.float32)


class Table:
    def __init__(self, groups, tensor):
        self.shape = (groups, tensor)
        self.columns = []
        self.size = 0

    def add(self, entry):
        block = np.array([[entry(g, z) for z in range(self.shape[1])] for g in range(self.shape[0])], np.int32)
        at = self.size
        self.columns.append(block)
        self.size += block.shape[2]
        return at

    def mine(self):
        whole = jnp.asarray(np.concatenate(self.columns, axis=2))
        row = lax.dynamic_slice(
            whole, (lax.axis_index("groups"), lax.axis_index("tensor"), 0), (1, 1, self.size)
        )
        return row.reshape(self.size)


HBM = pl.BlockSpec(memory_space=pltpu.HBM)
VMEM = pl.BlockSpec(memory_space=pltpu.VMEM)
SMEM = pl.BlockSpec(memory_space=pltpu.SMEM)
ANY = pl.BlockSpec(memory_space=pl.ANY)


def rows_at(ref, place, unit, offset, size):
    return ref.at[pl.ds(pl.multiple_of(place * unit + offset, 8), size)]


def project_kernel(at, count, tile, tab, g, l, p, *refs):
    out, g_in, l_in, p_in, w, sem, p_sem = refs[-7:]
    rank, width = p.shape
    half = tile // 2
    fetch = pltpu.make_async_copy(p, p_in, p_sem)
    fetch.start()
    copies = []
    for i in range(count):
        pair = [
            pltpu.make_async_copy(rows_at(x, tab[at + i], GRAIN, 0, tile), to.at[i], sem.at[n, i])
            for n, (x, to) in enumerate(((g, g_in), (l, l_in)))
        ]
        for copy in pair:
            copy.start()
        copies.append(pair)
    if len(refs) > 7:
        add = pltpu.make_async_copy(refs[0], out, p_sem)
    fetch.wait()
    if len(refs) > 7:
        add.start()
    high, low = (x.T for x in halves(p_in[...]))
    none = jnp.zeros_like(high)
    w[0:width] = jnp.concatenate([high, none, low, none], axis=1)
    w[width:] = jnp.concatenate([none, high, none, low], axis=1)
    if len(refs) > 7:
        add.wait()
    for i in range(count):
        for copy in copies[i]:
            copy.wait()
        difference = g_in[i] - l_in[i].astype(jnp.float32)
        high, low = halves(jnp.concatenate([difference[:half], difference[half:]], axis=1))
        wide = dot(high, w[...])
        mine = wide[:, 0 : 2 * rank] + wide[:, 2 * rank :] + dot(low, w[:, 0 : 2 * rank])
        rows = slice(i * half, (i + 1) * half)
        out[rows] = mine + out[rows] if len(refs) > 7 else mine


def project(tab, at, count, tile, global_embed, local_embed, projection_t, *got):
    width = global_embed.shape[1]
    rank = projection_t.shape[0]
    return pl.pallas_call(
        functools.partial(project_kernel, at, count, tile),
        in_specs=[SMEM, HBM, HBM, HBM] + [ANY] * len(got),
        out_specs=VMEM,
        out_shape=jax.ShapeDtypeStruct((count * tile // 2, 2 * rank), jnp.float32),
        scratch_shapes=[
            pltpu.VMEM((count, tile, width), jnp.float32),
            pltpu.VMEM((count, tile, width), jnp.bfloat16),
            pltpu.VMEM((rank, width), jnp.float32),
            pltpu.VMEM((2 * width, 4 * rank), jnp.bfloat16),
            pltpu.SemaphoreType.DMA((2, count)),
            pltpu.SemaphoreType.DMA(()),
        ],
        compiler_params=PARAMS,
        cost_estimate=COST,
        name="project",
    )(tab, global_embed, local_embed, projection_t, *got)


def update_kernel(at, unit, sub, subs, depth, parts, delta_of, extra, fixed, scratch, tab, *refs):
    far, (g, m) = refs[:extra], refs[extra : extra + 2]
    refs, scratch = refs[: len(refs) - scratch - fixed], refs[len(refs) - scratch - fixed :]
    new_g, new_m, g_in, m_in, g_out, m_out, packed, sem, source_sem, constant_sem = refs[-10:]
    near, scratch = scratch[:fixed], scratch[fixed:]
    count = parts

    def incoming(i, j):
        place, n = tab[at + count + i], i * subs + j
        return [
            pltpu.make_async_copy(rows_at(x, place, unit, j * sub, sub), to.at[n], sem.at[k, n])
            for k, (x, to) in enumerate(((g, g_in), (m, m_in)))
        ]

    def outgoing(i, j):
        place, n = tab[at + count + i], i * subs + j
        return [
            pltpu.make_async_copy(x.at[n], rows_at(to, place, unit, j * sub, sub), sem.at[2 + k, n])
            for k, (x, to) in enumerate(((g_out, new_g), (m_out, new_m)))
        ]

    def when_there(i, step):
        pl.when(tab[at + i] == 1)(step)

    def brought(i, source):
        here = pl.ds(pl.multiple_of(tab[at + 3 * count + i] * depth, 8), depth)
        return pltpu.make_async_copy(far[source].at[here], packed.at[i], source_sem.at[i])

    constant = [pltpu.make_async_copy(x, to, constant_sem) for x, to in zip(far[extra - fixed :], near)]
    for copy in constant:
        copy.start()
    for i in range(count):

        @functools.partial(when_there, i)
        def _(i=i):
            for n in range(extra - fixed):

                @pl.when(tab[at + 2 * count + i] == n)
                def _(n=n):
                    brought(i, n).start()

            for j in range(subs):
                for copy in incoming(i, j):
                    copy.start()

    for copy in constant:
        copy.wait()
    delta = delta_of(scratch, near)
    for i in range(count):

        @functools.partial(when_there, i)
        def _(i=i):
            brought(i, 0).wait()
            change = delta(packed.at[i])
            for j in range(subs):
                n = i * subs + j
                for copy in incoming(i, j):
                    copy.wait()
                weights = g_in[n]
                g_out[n], m_out[n] = nesterov(weights, m_in[n], change(j, weights))
                for copy in outgoing(i, j):
                    copy.start()

    for i in range(count):

        @functools.partial(when_there, i)
        def _(i=i):
            for j in range(subs):
                for copy in outgoing(i, j):
                    copy.wait()


def update(
    tab, at, unit, sub, subs, depth, parts, delta_of, sources, constants, weights, momentum, before, scratch, name
):
    rows, width = weights.shape
    extra = [] if before is None else list(before)
    count = parts * subs
    inputs = [*sources, *constants]
    where = 3 + len(inputs)
    return pl.pallas_call(
        functools.partial(
            update_kernel, at, unit, sub, subs, depth, parts, delta_of, len(inputs), len(constants), len(scratch)
        ),
        in_specs=[SMEM] + [ANY] * len(inputs) + [HBM] * (2 + len(extra)),
        out_specs=[HBM, HBM],
        out_shape=[jax.ShapeDtypeStruct((rows, width), jnp.float32)] * 2,
        input_output_aliases={} if before is None else {where: 0, where + 1: 1},
        scratch_shapes=[pltpu.VMEM((count, sub, width), jnp.float32)] * 4
        + [pltpu.VMEM((parts, depth, sources[0].shape[1]), jnp.float32)]
        + [pltpu.SemaphoreType.DMA((4, count)), pltpu.SemaphoreType.DMA((parts,)), pltpu.SemaphoreType.DMA(())]
        + [pltpu.VMEM(x.shape, x.dtype) for x in constants]
        + scratch,
        compiler_params=PARAMS,
        cost_estimate=COST,
        name=name,
    )(tab, *inputs, weights, momentum, *extra)


def embed_update(tab, at, tile, parts, sources, projection_t, weights, momentum, groups, before):
    width = weights.shape[1]
    rank = projection_t.shape[0]
    half = tile // 2

    def delta_of(scratch, refs):
        (w,) = scratch
        high, low = halves(refs[0][...])
        w[...] = jnp.zeros_like(w)
        for j in range(2):
            w[j, j * rank : (j + 1) * rank] = high
            w[j, (2 + j) * rank : (3 + j) * rank] = high
            w[j, (4 + j) * rank : (5 + j) * rank] = low

        def delta(packed):
            high, low = halves(packed[...] * (1 / groups))
            parts = jnp.concatenate([high, low, high], axis=1)
            return lambda j, weights: dot(parts, w[j])

        return delta

    scratch = [pltpu.VMEM((2, 6 * rank, width), jnp.bfloat16)]
    return update(
        tab, at, GRAIN, half, 2, half, parts, delta_of, sources, [projection_t], weights, momentum, before, scratch,
        "embed_update",
    )


def layer_update(tab, at, parts, sources, weights, momentum, groups, before):
    def delta_of(scratch, refs):
        return lambda packed: lambda j, weights: weights - packed[...] * (1 / groups)

    return update(
        tab, at, UNIT, UNIT, 1, UNIT, parts, delta_of, sources, [], weights, momentum, before, [], "layer_update"
    )


def widen_kernel(at, sizes, added, tab, l, *refs):
    got, outs, (l_in, sem), near = refs[:added], refs[added : -2 - added], refs[-2 - added :][:2], refs[len(refs) - added :]
    copies = [pltpu.make_async_copy(rows_at(l, tab[at], UNIT, 0, sum(sizes)), l_in, sem.at[0])]
    copies += [pltpu.make_async_copy(x, to, sem.at[1]) for x, to in zip(got, near)]
    for copy in copies:
        copy.start()
    for copy in copies:
        copy.wait()
    first = 0
    for out, size in zip(outs, sizes):
        value = l_in[first : first + size].astype(jnp.float32)
        out[...] = value + near[0][first : first + size] if added else value
        first += size


def widen(tab, at, sizes, local, *got):
    width = local.shape[1]
    return pl.pallas_call(
        functools.partial(widen_kernel, at, sizes, len(got)),
        in_specs=[SMEM, HBM] + [ANY] * len(got),
        out_specs=[VMEM] * len(sizes),
        out_shape=[jax.ShapeDtypeStruct((size, width), jnp.float32) for size in sizes],
        scratch_shapes=[pltpu.VMEM((sum(sizes), width), jnp.bfloat16), pltpu.SemaphoreType.DMA((2,))]
        + [pltpu.VMEM(x.shape, x.dtype) for x in got],
        compiler_params=PARAMS,
        cost_estimate=COST,
        name="widen",
    )(tab, local, *got)


class Order:
    def __init__(self):
        self.last = None

    def after(self, x):
        if self.last is None:
            return x
        return lax.optimization_barrier((x, self.last))[0]

    def done(self, x):
        self.last = x[0] if isinstance(x, (list, tuple)) else x
        return x


def swap_groups(x, bit):
    return lax.ppermute(x, "groups", [(g, g ^ bit) for g in range(4)])


def shift(x, step):
    pairs = []
    for g in range(4):
        for z in range(4):
            to = z + 1 if g % 2 == 0 else z - 1
            first = z if g % 2 == 0 else 3 - z
            if 0 <= to < 4 and first >= step:
                pairs.append((g * 4 + z, g * 4 + to))
    return lax.ppermute(x, ("groups", "tensor"), pairs)


def plain(
    global_layer, local_layer, layer_momentum, global_embed, local_embed, embed_momentum, projection
):
    groups = lax.axis_size("groups")
    exact = {"precision": lax.Precision.HIGHEST, "preferred_element_type": jnp.float32}
    projected = jnp.dot(global_embed - local_embed[0].astype(jnp.float32), projection, **exact)
    projected = lax.psum(projected, ("groups", "tensor")) / groups
    layer_delta = lax.psum(global_layer - local_layer[0].astype(jnp.float32), "groups") / groups
    embed_delta = jnp.dot(projected, projection.T, **exact)
    return (
        *nesterov(global_layer, layer_momentum, layer_delta),
        *nesterov(global_embed, embed_momentum, embed_delta),
    )


def body(
    global_layer, local_layer, layer_momentum, global_embed, local_embed, embed_momentum, projection
):
    groups = lax.axis_size("groups")
    tensor = lax.axis_size("tensor")
    rows, width = global_embed.shape
    weights = global_layer.reshape(-1, global_layer.shape[-1])
    units = weights.shape[0] // UNIT // 2
    grains = rows // (8 * GRAIN)
    whole = rows % (8 * GRAIN) == 0 and 8 <= grains <= 125 and weights.shape[0] % (2 * UNIT) == 0 and units == 6
    if not whole or (groups, tensor) != (4, 4) or width % 256 or projection.shape[1] != 64:
        return plain(
            global_layer, local_layer, layer_momentum, global_embed, local_embed, embed_momentum, projection
        )
    projection_t = projection.T
    embed_local = local_embed[0]
    momentum = layer_momentum.reshape(weights.shape)
    local = local_layer[0].reshape(weights.shape)
    table = Table(groups, tensor)
    chunks = [grains * 14 // 25]
    chunks.append(grains - sum(chunks))
    tiles = [n * GRAIN for n in chunks]
    bases = [0, 8 * chunks[0]]

    def core(g):
        return g % 2

    def place(c, h, k):
        return bases[c] + (h * 4 + k) * chunks[c]

    p_send = [table.add(lambda g, z, c=c: [place(c, 1 - core(g), k) for k in range(4)]) for c in range(2)]
    p_keep = [table.add(lambda g, z, c=c: [place(c, core(g), k) for k in range(4)]) for c in range(2)]

    def blocks_at(c, first):
        def entry(g, z):
            blocks = []
            for n in range(4):
                for h, k in ((core(g), z - n), (1 - core(g), z + n)):
                    k = 2 * z - k if core(g) else k
                    if n or h == core(g):
                        blocks.append((len(blocks), h, k))
            beside = [b for b in blocks[1:3] if 0 <= b[2] < 4][0]
            early = [blocks[0], beside]
            turn = early if first else [b for b in blocks if b not in early and 0 <= b[2] < 4]
            parts = [(place(c, h ^ half, k), n if first else n - 1, half) for n, h, k in turn for half in (0, 1)]
            return [1] * len(parts) + [p for column in zip(*parts) for p in column]

        return table.add(entry)

    near = [blocks_at(c, True) for c in range(2)]
    far = [blocks_at(c, False) for c in range(2)]
    pieces = [4, 2]
    firsts = [sum(pieces[:n]) for n in range(len(pieces))]
    l_send = table.add(lambda g, z: [(1 - core(g)) * units])
    l_keep = table.add(lambda g, z: [core(g) * units])

    l_both = [
        table.add(
            lambda g, z, f=f, n=n: [1] * (2 * n)
            + [h * units + f + u for h in (core(g), 1 - core(g)) for u in range(n)]
            + [source for source in (0, 1) for _ in range(n)]
            + [u for _ in (0, 1) for u in range(n)]
        )
        for f, n in zip(firsts, pieces)
    ]
    tab = table.mine()
    order = Order()

    def run(kernel, at, *args):
        return order.done(kernel(order.after(tab), at, *args))

    def add(a, b):
        return order.done(order.after(a) + b)

    def wait(x):
        return order.done(order.after(x))

    embed = (global_embed, embed_local, projection_t)
    state = {"embed": None, "layer": None}
    sizes = [n * UNIT for n in pieces]
    l_got, l_total, l_other = ([None] * len(pieces) for _ in range(3))
    sent, kept, summed, whole_block = ([None] * 2 for _ in range(4))
    came = [[None] * 3, [None] * 3]
    other = [[None] * 3, [None] * 3]

    def layer_send(n):
        l_got[n] = swap_groups(order.after(chip[n]), 2)

    def layer_sum(n):
        l_total[n] = add(chip[n], l_got[n])
        l_other[n] = swap_groups(l_total[n], 1)

    def layer_finish(n):
        sources = (l_total[n], l_other[n])
        state["layer"] = run(
            layer_update, l_both[n], 2 * pieces[n], sources, weights, momentum, groups, state["layer"]
        )

    def project_send(c):
        sent[c] = swap_groups(run(project, p_send[c], 4, tiles[c], *embed), 1)

    def project_keep(c):
        chip = run(project, p_keep[c], 4, tiles[c], *embed, sent[c])
        chip = chip.reshape((4, -1) + chip.shape[1:])
        if c == 1:
            kept[c] = lax.psum_scatter(chip, "tensor", scatter_dimension=0)
        else:
            kept[c] = lax.all_to_all(chip, "tensor", 0, 0)

    def far_send(c):
        kept[c] = wait(kept[c])
        if c == 0:
            kept[c] = order.done((kept[c][0] + kept[c][1]) + (kept[c][2] + kept[c][3]))
        kept[c] = kept[c].reshape(-1, kept[c].shape[-1])
        summed[c] = swap_groups(kept[c], 2)

    def far_sum(c):
        summed[c] = add(kept[c], summed[c])
        other_half = swap_groups(summed[c], 1)
        whole_block[c] = order.done(jnp.concatenate([order.after(summed[c]), other_half]))
        came[c][0] = shift(whole_block[c], 0)

    def step(c, n):
        came[c][n] = wait(came[c][n])
        if n < 2:
            came[c][n + 1] = shift(came[c][n], n + 1)
        other[c][n] = swap_groups(came[c][n], 1)

    def finish(c, at, *sources):
        state["embed"] = run(
            embed_update, at, tiles[c], 4, sources, projection_t, global_embed, embed_momentum, groups,
            state["embed"],
        )

    l_away = swap_groups(run(widen, l_send, [sum(sizes)], local)[0], 1)
    project_send(0)
    chip = run(widen, l_keep, sizes, local, l_away)
    layer_send(0)
    project_keep(0)
    project_send(1)
    project_keep(1)
    layer_sum(0)
    layer_finish(0)
    far_send(0)
    far_sum(0)
    far_send(1)
    step(0, 0)
    far_sum(1)
    finish(0, near[0], whole_block[0], came[0][0], other[0][0])
    step(0, 1)
    step(1, 0)
    layer_send(1)
    finish(1, near[1], whole_block[1], came[1][0], other[1][0])
    step(0, 2)
    step(1, 1)
    finish(0, far[0], came[0][0], other[0][0], came[0][1], other[0][1], came[0][2], other[0][2])
    layer_sum(1)
    step(1, 2)
    finish(1, far[1], came[1][0], other[1][0], came[1][1], other[1][1], came[1][2], other[1][2])
    layer_finish(1)
    new_layer, new_layer_momentum = (x.reshape(global_layer.shape) for x in state["layer"])
    return (new_layer, new_layer_momentum, *state["embed"])


def solution(mesh):
    in_specs = (
        P(None, "tensor", "shards"),
        P("groups", None, "tensor", "shards"),
        P(None, "tensor", "shards"),
        P("shards", "tensor"),
        P("groups", "shards", "tensor"),
        P("shards", "tensor"),
        P("tensor", None),
    )
    out_specs = (
        P(None, "tensor", "shards"),
        P(None, "tensor", "shards"),
        P("shards", "tensor"),
        P("shards", "tensor"),
    )
    return jax.shard_map(body, mesh=mesh, in_specs=in_specs, out_specs=out_specs, check_vma=False)
```

```python
import functools

import jax
import jax.numpy as jnp
import numpy as np
from jax import lax
from jax.experimental import pallas as pl
from jax.experimental.pallas import tpu as pltpu
from jax.sharding import PartitionSpec as P

momentum_rate = 0.9
outer_rate = 0.7
GRAIN = 16
UNIT = 176
COST = pl.CostEstimate(flops=0, bytes_accessed=0, transcendentals=0)
PARAMS = pltpu.CompilerParams(vmem_limit_bytes=53 * 1024 * 1024)


def nesterov(weights, momentum, delta):
    moved = momentum_rate * momentum + delta
    return (weights - outer_rate * (delta + momentum_rate * moved), moved)


def halves(value):
    high = value.astype(jnp.bfloat16)
    return high, (value - high.astype(jnp.float32)).astype(jnp.bfloat16)


def dot(a, b):
    return jnp.dot(a, b, preferred_element_type=jnp.float32)


class Table:
    def __init__(self, groups, tensor):
        self.shape = (groups, tensor)
        self.columns = []
        self.size = 0

    def add(self, entry):
        block = np.array([[entry(g, z) for z in range(self.shape[1])] for g in range(self.shape[0])], np.int32)
        at = self.size
        self.columns.append(block)
        self.size += block.shape[2]
        return at

    def mine(self):
        whole = jnp.asarray(np.concatenate(self.columns, axis=2))
        row = lax.dynamic_slice(
            whole, (lax.axis_index("groups"), lax.axis_index("tensor"), 0), (1, 1, self.size)
        )
        return row.reshape(self.size)


HBM = pl.BlockSpec(memory_space=pltpu.HBM)
VMEM = pl.BlockSpec(memory_space=pltpu.VMEM)
SMEM = pl.BlockSpec(memory_space=pltpu.SMEM)
ANY = pl.BlockSpec(memory_space=pl.ANY)


def rows_at(ref, place, unit, offset, size):
    return ref.at[pl.ds(pl.multiple_of(place * unit + offset, 8), size)]


def project_kernel(at, count, tile, tab, g, l, p, *refs):
    out, g_in, l_in, p_in, w, sem, p_sem = refs[-7:]
    rank, width = p.shape
    half = tile // 2
    fetch = pltpu.make_async_copy(p, p_in, p_sem)
    fetch.start()
    copies = []
    for i in range(count):
        pair = [
            pltpu.make_async_copy(rows_at(x, tab[at + i], GRAIN, 0, tile), to.at[i], sem.at[n, i])
            for n, (x, to) in enumerate(((g, g_in), (l, l_in)))
        ]
        for copy in pair:
            copy.start()
        copies.append(pair)
    fetch.wait()
    high, low = (x.T for x in halves(p_in[...]))
    none = jnp.zeros_like(high)
    w[0:width] = jnp.concatenate([high, none, low, none], axis=1)
    w[width:] = jnp.concatenate([none, high, none, low], axis=1)
    for i in range(count):
        for copy in copies[i]:
            copy.wait()
        difference = g_in[i] - l_in[i].astype(jnp.float32)
        high, low = halves(jnp.concatenate([difference[:half], difference[half:]], axis=1))
        wide = dot(high, w[...])
        mine = wide[:, 0 : 2 * rank] + wide[:, 2 * rank :] + dot(low, w[:, 0 : 2 * rank])
        rows = slice(i * half, (i + 1) * half)
        out[rows] = mine + refs[0][rows] if len(refs) > 7 else mine


def project(tab, at, count, tile, global_embed, local_embed, projection_t, *got):
    width = global_embed.shape[1]
    rank = projection_t.shape[0]
    return pl.pallas_call(
        functools.partial(project_kernel, at, count, tile),
        in_specs=[SMEM, HBM, HBM, HBM] + [VMEM] * len(got),
        out_specs=VMEM,
        out_shape=jax.ShapeDtypeStruct((count * tile // 2, 2 * rank), jnp.float32),
        scratch_shapes=[
            pltpu.VMEM((count, tile, width), jnp.float32),
            pltpu.VMEM((count, tile, width), jnp.bfloat16),
            pltpu.VMEM((rank, width), jnp.float32),
            pltpu.VMEM((2 * width, 4 * rank), jnp.bfloat16),
            pltpu.SemaphoreType.DMA((2, count)),
            pltpu.SemaphoreType.DMA(()),
        ],
        compiler_params=PARAMS,
        cost_estimate=COST,
        name="project",
    )(tab, global_embed, local_embed, projection_t, *got)


def update_kernel(at, unit, sub, subs, depth, parts, delta_of, extra, fixed, scratch, tab, *refs):
    far, (g, m) = refs[:extra], refs[extra : extra + 2]
    refs, scratch = refs[: len(refs) - scratch - fixed], refs[len(refs) - scratch - fixed :]
    new_g, new_m, g_in, m_in, g_out, m_out, packed, sem, source_sem, constant_sem = refs[-10:]
    near, scratch = scratch[:fixed], scratch[fixed:]
    count = parts

    def incoming(i, j):
        place, n = tab[at + count + i], i * subs + j
        return [
            pltpu.make_async_copy(rows_at(x, place, unit, j * sub, sub), to.at[n], sem.at[k, n])
            for k, (x, to) in enumerate(((g, g_in), (m, m_in)))
        ]

    def outgoing(i, j):
        place, n = tab[at + count + i], i * subs + j
        return [
            pltpu.make_async_copy(x.at[n], rows_at(to, place, unit, j * sub, sub), sem.at[2 + k, n])
            for k, (x, to) in enumerate(((g_out, new_g), (m_out, new_m)))
        ]

    def when_there(i, step):
        pl.when(tab[at + i] == 1)(step)

    def brought(i, source):
        here = pl.ds(pl.multiple_of(tab[at + 3 * count + i] * depth, 8), depth)
        return pltpu.make_async_copy(far[source].at[here], packed.at[i], source_sem.at[i])

    constant = [pltpu.make_async_copy(x, to, constant_sem) for x, to in zip(far[extra - fixed :], near)]
    for copy in constant:
        copy.start()
    for i in range(count):

        @functools.partial(when_there, i)
        def _(i=i):
            for n in range(extra - fixed):

                @pl.when(tab[at + 2 * count + i] == n)
                def _(n=n):
                    brought(i, n).start()

            for j in range(subs):
                for copy in incoming(i, j):
                    copy.start()

    for copy in constant:
        copy.wait()
    delta = delta_of(scratch, near)
    for i in range(count):

        @functools.partial(when_there, i)
        def _(i=i):
            brought(i, 0).wait()
            change = delta(packed.at[i])
            for j in range(subs):
                n = i * subs + j
                for copy in incoming(i, j):
                    copy.wait()
                weights = g_in[n]
                g_out[n], m_out[n] = nesterov(weights, m_in[n], change(j, weights))
                for copy in outgoing(i, j):
                    copy.start()

    for i in range(count):

        @functools.partial(when_there, i)
        def _(i=i):
            for j in range(subs):
                for copy in outgoing(i, j):
                    copy.wait()


def update(
    tab, at, unit, sub, subs, depth, parts, delta_of, sources, constants, weights, momentum, before, scratch, name
):
    rows, width = weights.shape
    extra = [] if before is None else list(before)
    count = parts * subs
    inputs = [*sources, *constants]
    where = 3 + len(inputs)
    return pl.pallas_call(
        functools.partial(
            update_kernel, at, unit, sub, subs, depth, parts, delta_of, len(inputs), len(constants), len(scratch)
        ),
        in_specs=[SMEM] + [ANY] * len(inputs) + [HBM] * (2 + len(extra)),
        out_specs=[HBM, HBM],
        out_shape=[jax.ShapeDtypeStruct((rows, width), jnp.float32)] * 2,
        input_output_aliases={} if before is None else {where: 0, where + 1: 1},
        scratch_shapes=[pltpu.VMEM((count, sub, width), jnp.float32)] * 4
        + [pltpu.VMEM((parts, depth, sources[0].shape[1]), jnp.float32)]
        + [pltpu.SemaphoreType.DMA((4, count)), pltpu.SemaphoreType.DMA((parts,)), pltpu.SemaphoreType.DMA(())]
        + [pltpu.VMEM(x.shape, x.dtype) for x in constants]
        + scratch,
        compiler_params=PARAMS,
        cost_estimate=COST,
        name=name,
    )(tab, *inputs, weights, momentum, *extra)


def embed_update(tab, at, tile, parts, sources, projection_t, weights, momentum, groups, before):
    width = weights.shape[1]
    rank = projection_t.shape[0]
    half = tile // 2

    def delta_of(scratch, refs):
        (w,) = scratch
        high, low = halves(refs[0][...])
        w[...] = jnp.zeros_like(w)
        for j in range(2):
            w[j, j * rank : (j + 1) * rank] = high
            w[j, (2 + j) * rank : (3 + j) * rank] = high
            w[j, (4 + j) * rank : (5 + j) * rank] = low

        def delta(packed):
            high, low = halves(packed[...] * (1 / groups))
            parts = jnp.concatenate([high, low, high], axis=1)
            return lambda j, weights: dot(parts, w[j])

        return delta

    scratch = [pltpu.VMEM((2, 6 * rank, width), jnp.bfloat16)]
    return update(
        tab, at, GRAIN, half, 2, half, parts, delta_of, sources, [projection_t], weights, momentum, before, scratch,
        "embed_update",
    )


def layer_update(tab, at, parts, sources, weights, momentum, groups, before):
    def delta_of(scratch, refs):
        return lambda packed: lambda j, weights: weights - packed[...] * (1 / groups)

    return update(
        tab, at, UNIT, UNIT, 1, UNIT, parts, delta_of, sources, [], weights, momentum, before, [], "layer_update"
    )


def widen_kernel(at, sizes, tab, l, *refs):
    *got, l_in, sem = refs
    got, outs = got[: len(got) - len(sizes)], got[len(got) - len(sizes) :]
    copy = pltpu.make_async_copy(rows_at(l, tab[at], UNIT, 0, sum(sizes)), l_in, sem)
    copy.start()
    copy.wait()
    first = 0
    for out, size in zip(outs, sizes):
        value = l_in[first : first + size].astype(jnp.float32)
        out[...] = value + got[0][first : first + size] if got else value
        first += size


def widen(tab, at, sizes, local, *got):
    width = local.shape[1]
    return pl.pallas_call(
        functools.partial(widen_kernel, at, sizes),
        in_specs=[SMEM, HBM] + [VMEM] * len(got),
        out_specs=[VMEM] * len(sizes),
        out_shape=[jax.ShapeDtypeStruct((size, width), jnp.float32) for size in sizes],
        scratch_shapes=[pltpu.VMEM((sum(sizes), width), jnp.bfloat16), pltpu.SemaphoreType.DMA(())],
        compiler_params=PARAMS,
        cost_estimate=COST,
        name="widen",
    )(tab, local, *got)


class Order:
    def __init__(self):
        self.last = None

    def after(self, x):
        if self.last is None:
            return x
        return lax.optimization_barrier((x, self.last))[0]

    def done(self, x):
        self.last = x[0] if isinstance(x, (list, tuple)) else x
        return x


def swap_groups(x, bit):
    return lax.ppermute(x, "groups", [(g, g ^ bit) for g in range(4)])


def shift(x, step):
    pairs = []
    for g in range(4):
        for z in range(4):
            to = z + 1 if g % 2 == 0 else z - 1
            first = z if g % 2 == 0 else 3 - z
            if 0 <= to < 4 and first >= step:
                pairs.append((g * 4 + z, g * 4 + to))
    return lax.ppermute(x, ("groups", "tensor"), pairs)


def plain(
    global_layer, local_layer, layer_momentum, global_embed, local_embed, embed_momentum, projection
):
    groups = lax.axis_size("groups")
    exact = {"precision": lax.Precision.HIGHEST, "preferred_element_type": jnp.float32}
    projected = jnp.dot(global_embed - local_embed[0].astype(jnp.float32), projection, **exact)
    projected = lax.psum(projected, ("groups", "tensor")) / groups
    layer_delta = lax.psum(global_layer - local_layer[0].astype(jnp.float32), "groups") / groups
    embed_delta = jnp.dot(projected, projection.T, **exact)
    return (
        *nesterov(global_layer, layer_momentum, layer_delta),
        *nesterov(global_embed, embed_momentum, embed_delta),
    )


def body(
    global_layer, local_layer, layer_momentum, global_embed, local_embed, embed_momentum, projection
):
    groups = lax.axis_size("groups")
    tensor = lax.axis_size("tensor")
    rows, width = global_embed.shape
    weights = global_layer.reshape(-1, global_layer.shape[-1])
    units = weights.shape[0] // UNIT // 2
    grains = rows // (8 * GRAIN)
    whole = rows % (8 * GRAIN) == 0 and 8 <= grains <= 125 and weights.shape[0] % (2 * UNIT) == 0 and units == 6
    if not whole or (groups, tensor) != (4, 4) or width % 256 or projection.shape[1] != 64:
        return plain(
            global_layer, local_layer, layer_momentum, global_embed, local_embed, embed_momentum, projection
        )
    projection_t = projection.T
    embed_local = local_embed[0]
    momentum = layer_momentum.reshape(weights.shape)
    local = local_layer[0].reshape(weights.shape)
    table = Table(groups, tensor)
    chunks = [grains * 14 // 25]
    chunks.append(grains - sum(chunks))
    tiles = [n * GRAIN for n in chunks]
    bases = [0, 8 * chunks[0]]

    def core(g):
        return g % 2

    def place(c, h, k):
        return bases[c] + (h * 4 + k) * chunks[c]

    p_send = [table.add(lambda g, z, c=c: [place(c, 1 - core(g), k) for k in range(4)]) for c in range(2)]
    p_keep = [table.add(lambda g, z, c=c: [place(c, core(g), k) for k in range(4)]) for c in range(2)]

    def blocks_at(c, turn):
        def entry(g, z):
            blocks = []
            for n in range(4):
                for h, k in ((core(g), z - n), (1 - core(g), z + n)):
                    k = 2 * z - k if core(g) else k
                    if n or h == core(g):
                        blocks.append((len(blocks), h, k))
            there = [b for b in blocks if 0 <= b[2] < 4]
            taken = (there[:1], there[1:2], there[2:], there[:2])[turn]
            parts = [(place(c, h ^ half, k), n - (turn in (1, 2)), half) for n, h, k in taken for half in (0, 1)]
            return [1] * len(parts) + [p for column in zip(*parts) for p in column]

        return table.add(entry)

    own, beside, far, near = ([blocks_at(c, turn) for c in range(2)] for turn in range(4))
    pieces = [3, 3]
    firsts = [sum(pieces[:n]) for n in range(len(pieces))]
    l_send = table.add(lambda g, z: [(1 - core(g)) * units])
    l_keep = table.add(lambda g, z: [core(g) * units])


    def l_entry(g, z):
        parts = []
        for n, (f, size) in enumerate(zip(firsts, pieces)):
            for h in (0, 1):
                parts += [((core(g) ^ h) * units + f + u, 2 * n + h, u) for u in range(size)]
        return [1] * len(parts) + [p for column in zip(*parts) for p in column]

    l_all = table.add(l_entry)
    tab = table.mine()
    order = Order()

    def run(kernel, at, *args):
        return order.done(kernel(order.after(tab), at, *args))

    def add(a, b):
        return order.done(order.after(a) + b)

    def wait(x):
        return order.done(order.after(x))

    embed = (global_embed, embed_local, projection_t)
    state = {"embed": None, "layer": None}
    sizes = [n * UNIT for n in pieces]
    l_got, l_total, l_other = ([None] * len(pieces) for _ in range(3))
    sent, kept, summed, whole_block = ([None] * 2 for _ in range(4))
    came = [[None] * 3, [None] * 3]
    other = [[None] * 3, [None] * 3]

    def layer_send(n):
        l_got[n] = swap_groups(order.after(chip[n]), 2)

    def layer_sum(n):
        l_total[n] = add(chip[n], l_got[n])
        l_other[n] = swap_groups(l_total[n], 1)

    def layer_finish():
        sources = [x for pair in zip(l_total, l_other) for x in pair]
        state["layer"] = run(layer_update, l_all, 2 * units, sources, weights, momentum, groups, state["layer"])

    def project_send(c):
        sent[c] = swap_groups(run(project, p_send[c], 4, tiles[c], *embed), 1)

    def project_keep(c):
        chip = run(project, p_keep[c], 4, tiles[c], *embed, sent[c])
        chip = chip.reshape((4, -1) + chip.shape[1:])
        if c == 0:
            kept[c] = lax.psum_scatter(chip, "tensor", scatter_dimension=0)
        else:
            kept[c] = lax.all_to_all(chip, "tensor", 0, 0)

    def far_send(c):
        kept[c] = wait(kept[c])
        if c == 1:
            kept[c] = order.done((kept[c][0] + kept[c][1]) + (kept[c][2] + kept[c][3]))
        kept[c] = kept[c].reshape(-1, kept[c].shape[-1])
        summed[c] = swap_groups(kept[c], 2)

    def far_sum(c):
        summed[c] = add(kept[c], summed[c])
        whole_block[c] = swap_groups(summed[c], 1)

    def spread(c):
        whole_block[c] = order.done(jnp.concatenate([order.after(summed[c]), whole_block[c]]))
        came[c][0] = shift(whole_block[c], 0)

    def step(c, n):
        came[c][n] = wait(came[c][n])
        if n < 2:
            came[c][n + 1] = shift(came[c][n], n + 1)
        other[c][n] = swap_groups(came[c][n], 1)

    def finish(c, at, count, *sources):
        state["embed"] = run(
            embed_update, at[c], tiles[c], count, sources, projection_t, global_embed, embed_momentum, groups,
            state["embed"],
        )

    def received(c, steps):
        return [x for n in range(steps) for x in (came[c][n], other[c][n])]

    project_send(0)
    l_away = swap_groups(run(widen, l_send, [sum(sizes)], local)[0], 1)
    project_keep(0)
    project_send(1)
    chip = run(widen, l_keep, sizes, local, l_away)
    layer_send(0)
    project_keep(1)
    far_send(0)
    layer_sum(0)
    far_sum(0)
    spread(0)
    far_send(1)
    finish(0, own, 2, whole_block[0])
    step(0, 0)
    far_sum(1)
    spread(1)
    finish(0, beside, 2, *received(0, 1))
    step(0, 1)
    step(1, 0)
    layer_send(1)
    finish(1, near, 4, whole_block[1], *received(1, 1))
    step(0, 2)
    step(1, 1)
    finish(0, far, 4, *received(0, 3))
    step(1, 2)
    layer_sum(1)
    finish(1, far, 4, *received(1, 3))
    layer_finish()
    new_layer, new_layer_momentum = (x.reshape(global_layer.shape) for x in state["layer"])
    return (new_layer, new_layer_momentum, *state["embed"])


def solution(mesh):
    in_specs = (
        P(None, "tensor", "shards"),
        P("groups", None, "tensor", "shards"),
        P(None, "tensor", "shards"),
        P("shards", "tensor"),
        P("groups", "shards", "tensor"),
        P("shards", "tensor"),
        P("tensor", None),
    )
    out_specs = (
        P(None, "tensor", "shards"),
        P(None, "tensor", "shards"),
        P("shards", "tensor"),
        P("shards", "tensor"),
    )
    return jax.shard_map(body, mesh=mesh, in_specs=in_specs, out_specs=out_specs, check_vma=False)
```

```python
import functools

import jax
import jax.numpy as jnp
import numpy as np
from jax import lax
from jax.experimental import pallas as pl
from jax.experimental.pallas import tpu as pltpu
from jax.sharding import PartitionSpec as P

momentum_rate = 0.9
outer_rate = 0.7
GRAIN = 16
UNIT = 176
COST = pl.CostEstimate(flops=0, bytes_accessed=0, transcendentals=0)
PARAMS = pltpu.CompilerParams(vmem_limit_bytes=53 * 1024 * 1024)


def nesterov(weights, momentum, delta):
    moved = momentum_rate * momentum + delta
    return (weights - outer_rate * (delta + momentum_rate * moved), moved)


def halves(value):
    high = value.astype(jnp.bfloat16)
    return high, (value - high.astype(jnp.float32)).astype(jnp.bfloat16)


def dot(a, b):
    return jnp.dot(a, b, preferred_element_type=jnp.float32)


class Table:
    def __init__(self, groups, tensor):
        self.shape = (groups, tensor)
        self.columns = []
        self.size = 0

    def add(self, entry):
        block = np.array([[entry(g, z) for z in range(self.shape[1])] for g in range(self.shape[0])], np.int32)
        at = self.size
        self.columns.append(block)
        self.size += block.shape[2]
        return at

    def mine(self):
        whole = jnp.asarray(np.concatenate(self.columns, axis=2))
        row = lax.dynamic_slice(
            whole, (lax.axis_index("groups"), lax.axis_index("tensor"), 0), (1, 1, self.size)
        )
        return row.reshape(self.size)


HBM = pl.BlockSpec(memory_space=pltpu.HBM)
VMEM = pl.BlockSpec(memory_space=pltpu.VMEM)
SMEM = pl.BlockSpec(memory_space=pltpu.SMEM)
ANY = pl.BlockSpec(memory_space=pl.ANY)


def rows_at(ref, place, unit, offset, size):
    return ref.at[pl.ds(pl.multiple_of(place * unit + offset, 8), size)]


def project_kernel(at, count, tile, tab, g, l, p, *refs):
    out, g_in, l_in, p_in, w, sem, p_sem = refs[-7:]
    rank, width = p.shape
    half = tile // 2
    fetch = pltpu.make_async_copy(p, p_in, p_sem)
    fetch.start()
    copies = []
    for i in range(count):
        pair = [
            pltpu.make_async_copy(rows_at(x, tab[at + i], GRAIN, 0, tile), to.at[i], sem.at[n, i])
            for n, (x, to) in enumerate(((g, g_in), (l, l_in)))
        ]
        for copy in pair:
            copy.start()
        copies.append(pair)
    fetch.wait()
    high, low = (x.T for x in halves(p_in[...]))
    none = jnp.zeros_like(high)
    w[0:width] = jnp.concatenate([high, none, low, none], axis=1)
    w[width:] = jnp.concatenate([none, high, none, low], axis=1)
    for i in range(count):
        for copy in copies[i]:
            copy.wait()
        difference = g_in[i] - l_in[i].astype(jnp.float32)
        high, low = halves(jnp.concatenate([difference[:half], difference[half:]], axis=1))
        wide = dot(high, w[...])
        mine = wide[:, 0 : 2 * rank] + wide[:, 2 * rank :] + dot(low, w[:, 0 : 2 * rank])
        rows = slice(i * half, (i + 1) * half)
        out[rows] = mine + refs[0][rows] if len(refs) > 7 else mine


def project(tab, at, count, tile, global_embed, local_embed, projection_t, *got):
    width = global_embed.shape[1]
    rank = projection_t.shape[0]
    return pl.pallas_call(
        functools.partial(project_kernel, at, count, tile),
        in_specs=[SMEM, HBM, HBM, HBM] + [VMEM] * len(got),
        out_specs=VMEM,
        out_shape=jax.ShapeDtypeStruct((count * tile // 2, 2 * rank), jnp.float32),
        scratch_shapes=[
            pltpu.VMEM((count, tile, width), jnp.float32),
            pltpu.VMEM((count, tile, width), jnp.bfloat16),
            pltpu.VMEM((rank, width), jnp.float32),
            pltpu.VMEM((2 * width, 4 * rank), jnp.bfloat16),
            pltpu.SemaphoreType.DMA((2, count)),
            pltpu.SemaphoreType.DMA(()),
        ],
        compiler_params=PARAMS,
        cost_estimate=COST,
        name="project",
    )(tab, global_embed, local_embed, projection_t, *got)


def update_kernel(at, unit, sub, subs, depth, parts, delta_of, extra, fixed, scratch, tab, *refs):
    far, (g, m) = refs[:extra], refs[extra : extra + 2]
    refs, scratch = refs[: len(refs) - scratch - fixed], refs[len(refs) - scratch - fixed :]
    new_g, new_m, g_in, m_in, g_out, m_out, packed, sem, source_sem, constant_sem = refs[-10:]
    near, scratch = scratch[:fixed], scratch[fixed:]
    count = parts

    def incoming(i, j):
        place, n = tab[at + count + i], i * subs + j
        return [
            pltpu.make_async_copy(rows_at(x, place, unit, j * sub, sub), to.at[n], sem.at[k, n])
            for k, (x, to) in enumerate(((g, g_in), (m, m_in)))
        ]

    def outgoing(i, j):
        place, n = tab[at + count + i], i * subs + j
        return [
            pltpu.make_async_copy(x.at[n], rows_at(to, place, unit, j * sub, sub), sem.at[2 + k, n])
            for k, (x, to) in enumerate(((g_out, new_g), (m_out, new_m)))
        ]

    def when_there(i, step):
        pl.when(tab[at + i] == 1)(step)

    def brought(i, source):
        here = pl.ds(pl.multiple_of(tab[at + 3 * count + i] * depth, 8), depth)
        return pltpu.make_async_copy(far[source].at[here], packed.at[i], source_sem.at[i])

    constant = [pltpu.make_async_copy(x, to, constant_sem) for x, to in zip(far[extra - fixed :], near)]
    for copy in constant:
        copy.start()
    for i in range(count):

        @functools.partial(when_there, i)
        def _(i=i):
            for n in range(extra - fixed):

                @pl.when(tab[at + 2 * count + i] == n)
                def _(n=n):
                    brought(i, n).start()

            for j in range(subs):
                for copy in incoming(i, j):
                    copy.start()

    for copy in constant:
        copy.wait()
    delta = delta_of(scratch, near)
    for i in range(count):

        @functools.partial(when_there, i)
        def _(i=i):
            brought(i, 0).wait()
            change = delta(packed.at[i])
            for j in range(subs):
                n = i * subs + j
                for copy in incoming(i, j):
                    copy.wait()
                weights = g_in[n]
                g_out[n], m_out[n] = nesterov(weights, m_in[n], change(j, weights))
                for copy in outgoing(i, j):
                    copy.start()

    for i in range(count):

        @functools.partial(when_there, i)
        def _(i=i):
            for j in range(subs):
                for copy in outgoing(i, j):
                    copy.wait()


def update(
    tab, at, unit, sub, subs, depth, parts, delta_of, sources, constants, weights, momentum, before, scratch, name
):
    rows, width = weights.shape
    extra = [] if before is None else list(before)
    count = parts * subs
    inputs = [*sources, *constants]
    where = 3 + len(inputs)
    return pl.pallas_call(
        functools.partial(
            update_kernel, at, unit, sub, subs, depth, parts, delta_of, len(inputs), len(constants), len(scratch)
        ),
        in_specs=[SMEM] + [ANY] * len(inputs) + [HBM] * (2 + len(extra)),
        out_specs=[HBM, HBM],
        out_shape=[jax.ShapeDtypeStruct((rows, width), jnp.float32)] * 2,
        input_output_aliases={} if before is None else {where: 0, where + 1: 1},
        scratch_shapes=[pltpu.VMEM((count, sub, width), jnp.float32)] * 4
        + [pltpu.VMEM((parts, depth, sources[0].shape[1]), jnp.float32)]
        + [pltpu.SemaphoreType.DMA((4, count)), pltpu.SemaphoreType.DMA((parts,)), pltpu.SemaphoreType.DMA(())]
        + [pltpu.VMEM(x.shape, x.dtype) for x in constants]
        + scratch,
        compiler_params=PARAMS,
        cost_estimate=COST,
        name=name,
    )(tab, *inputs, weights, momentum, *extra)


def embed_update(tab, at, tile, parts, sources, projection_t, weights, momentum, groups, before):
    width = weights.shape[1]
    rank = projection_t.shape[0]
    half = tile // 2

    def delta_of(scratch, refs):
        (w,) = scratch
        high, low = halves(refs[0][...])
        w[...] = jnp.zeros_like(w)
        for j in range(2):
            w[j, j * rank : (j + 1) * rank] = high
            w[j, (2 + j) * rank : (3 + j) * rank] = high
            w[j, (4 + j) * rank : (5 + j) * rank] = low

        def delta(packed):
            high, low = halves(packed[...] * (1 / groups))
            parts = jnp.concatenate([high, low, high], axis=1)
            return lambda j, weights: dot(parts, w[j])

        return delta

    scratch = [pltpu.VMEM((2, 6 * rank, width), jnp.bfloat16)]
    return update(
        tab, at, GRAIN, half, 2, half, parts, delta_of, sources, [projection_t], weights, momentum, before, scratch,
        "embed_update",
    )


def layer_update(tab, at, parts, sources, weights, momentum, groups, before):
    def delta_of(scratch, refs):
        return lambda packed: lambda j, weights: weights - packed[...] * (1 / groups)

    return update(
        tab, at, UNIT, UNIT, 1, UNIT, parts, delta_of, sources, [], weights, momentum, before, [], "layer_update"
    )


def widen_kernel(at, sizes, tab, l, *refs):
    *got, l_in, sem = refs
    got, outs = got[: len(got) - len(sizes)], got[len(got) - len(sizes) :]
    copy = pltpu.make_async_copy(rows_at(l, tab[at], UNIT, 0, sum(sizes)), l_in, sem)
    copy.start()
    copy.wait()
    first = 0
    for out, size in zip(outs, sizes):
        value = l_in[first : first + size].astype(jnp.float32)
        out[...] = value + got[0][first : first + size] if got else value
        first += size


def widen(tab, at, sizes, local, *got):
    width = local.shape[1]
    return pl.pallas_call(
        functools.partial(widen_kernel, at, sizes),
        in_specs=[SMEM, HBM] + [VMEM] * len(got),
        out_specs=[VMEM] * len(sizes),
        out_shape=[jax.ShapeDtypeStruct((size, width), jnp.float32) for size in sizes],
        scratch_shapes=[pltpu.VMEM((sum(sizes), width), jnp.bfloat16), pltpu.SemaphoreType.DMA(())],
        compiler_params=PARAMS,
        cost_estimate=COST,
        name="widen",
    )(tab, local, *got)


class Order:
    def __init__(self):
        self.last = None

    def after(self, x):
        if self.last is None:
            return x
        return lax.optimization_barrier((x, self.last))[0]

    def done(self, x):
        self.last = x[0] if isinstance(x, (list, tuple)) else x
        return x


def swap_groups(x, bit):
    return lax.ppermute(x, "groups", [(g, g ^ bit) for g in range(4)])


def shift(x, step):
    pairs = []
    for g in range(4):
        for z in range(4):
            to = z + 1 if g % 2 == 0 else z - 1
            first = z if g % 2 == 0 else 3 - z
            if 0 <= to < 4 and first >= step:
                pairs.append((g * 4 + z, g * 4 + to))
    return lax.ppermute(x, ("groups", "tensor"), pairs)


def plain(
    global_layer, local_layer, layer_momentum, global_embed, local_embed, embed_momentum, projection
):
    groups = lax.axis_size("groups")
    exact = {"precision": lax.Precision.HIGHEST, "preferred_element_type": jnp.float32}
    projected = jnp.dot(global_embed - local_embed[0].astype(jnp.float32), projection, **exact)
    projected = lax.psum(projected, ("groups", "tensor")) / groups
    layer_delta = lax.psum(global_layer - local_layer[0].astype(jnp.float32), "groups") / groups
    embed_delta = jnp.dot(projected, projection.T, **exact)
    return (
        *nesterov(global_layer, layer_momentum, layer_delta),
        *nesterov(global_embed, embed_momentum, embed_delta),
    )


def body(
    global_layer, local_layer, layer_momentum, global_embed, local_embed, embed_momentum, projection
):
    groups = lax.axis_size("groups")
    tensor = lax.axis_size("tensor")
    rows, width = global_embed.shape
    weights = global_layer.reshape(-1, global_layer.shape[-1])
    units = weights.shape[0] // UNIT // 2
    grains = rows // (8 * GRAIN)
    whole = rows % (8 * GRAIN) == 0 and 8 <= grains <= 125 and weights.shape[0] % (2 * UNIT) == 0 and units == 6
    if not whole or (groups, tensor) != (4, 4) or width % 256 or projection.shape[1] != 64:
        return plain(
            global_layer, local_layer, layer_momentum, global_embed, local_embed, embed_momentum, projection
        )
    projection_t = projection.T
    embed_local = local_embed[0]
    momentum = layer_momentum.reshape(weights.shape)
    local = local_layer[0].reshape(weights.shape)
    table = Table(groups, tensor)
    chunks = [grains * 14 // 25]
    chunks.append(grains - sum(chunks))
    tiles = [n * GRAIN for n in chunks]
    bases = [0, 8 * chunks[0]]

    def core(g):
        return g % 2

    def place(c, h, k):
        return bases[c] + (h * 4 + k) * chunks[c]

    p_send = [table.add(lambda g, z, c=c: [place(c, 1 - core(g), k) for k in range(4)]) for c in range(2)]
    p_keep = [table.add(lambda g, z, c=c: [place(c, core(g), k) for k in range(4)]) for c in range(2)]

    def blocks_at(c, turn):
        def entry(g, z):
            blocks = []
            for n in range(4):
                for h, k in ((core(g), z - n), (1 - core(g), z + n)):
                    k = 2 * z - k if core(g) else k
                    if n or h == core(g):
                        blocks.append((len(blocks), h, k))
            there = [b for b in blocks if 0 <= b[2] < 4]
            taken = (there[:1], there[1:2], there[2:], there[:2])[turn]
            parts = [(place(c, h ^ half, k), n - (turn in (1, 2)), half) for n, h, k in taken for half in (0, 1)]
            return [1] * len(parts) + [p for column in zip(*parts) for p in column]

        return table.add(entry)

    own, beside, far, near = ([blocks_at(c, turn) for c in range(2)] for turn in range(4))
    pieces = [3, 3]
    firsts = [sum(pieces[:n]) for n in range(len(pieces))]
    l_send = table.add(lambda g, z: [(1 - core(g)) * units])
    l_keep = table.add(lambda g, z: [core(g) * units])


    def l_place(n):
        def entry(g, z):
            parts = [
                ((core(g) ^ h) * units + firsts[n] + u, h, u) for h in (0, 1) for u in range(pieces[n])
            ]
            return [1] * len(parts) + [p for column in zip(*parts) for p in column]

        return table.add(entry)

    l_place_of = [l_place(n) for n in range(len(pieces))]
    tab = table.mine()
    order = Order()

    def run(kernel, at, *args):
        return order.done(kernel(order.after(tab), at, *args))

    def add(a, b):
        return order.done(order.after(a) + b)

    def wait(x):
        return order.done(order.after(x))

    embed = (global_embed, embed_local, projection_t)
    state = {"embed": None, "layer": None}
    sizes = [n * UNIT for n in pieces]
    l_got, l_total, l_other = ([None] * len(pieces) for _ in range(3))
    sent, kept, summed, whole_block = ([None] * 2 for _ in range(4))
    came = [[None] * 3, [None] * 3]
    other = [[None] * 3, [None] * 3]

    def layer_send(n):
        l_got[n] = swap_groups(order.after(chip[n]), 2)

    def layer_sum(n):
        l_total[n] = add(chip[n], l_got[n])
        l_other[n] = swap_groups(l_total[n], 1)

    def layer_finish(n):
        sources = (l_total[n], l_other[n])
        state["layer"] = run(
            layer_update, l_place_of[n], 2 * pieces[n], sources, weights, momentum, groups, state["layer"]
        )

    def project_send(c):
        sent[c] = swap_groups(run(project, p_send[c], 4, tiles[c], *embed), 1)

    def project_keep(c):
        chip = run(project, p_keep[c], 4, tiles[c], *embed, sent[c])
        chip = chip.reshape((4, -1) + chip.shape[1:])
        kept[c] = lax.all_to_all(chip, "tensor", 0, 0)

    def far_send(c):
        kept[c] = wait(kept[c])
        kept[c] = order.done((kept[c][0] + kept[c][1]) + (kept[c][2] + kept[c][3]))
        kept[c] = kept[c].reshape(-1, kept[c].shape[-1])
        summed[c] = swap_groups(kept[c], 2)

    def far_sum(c):
        summed[c] = add(kept[c], summed[c])
        whole_block[c] = swap_groups(summed[c], 1)

    def spread(c):
        whole_block[c] = order.done(jnp.concatenate([order.after(summed[c]), whole_block[c]]))
        came[c][0] = shift(whole_block[c], 0)

    def step(c, n):
        came[c][n] = wait(came[c][n])
        if n < 2:
            came[c][n + 1] = shift(came[c][n], n + 1)
        other[c][n] = swap_groups(came[c][n], 1)

    def finish(c, at, count, *sources):
        state["embed"] = run(
            embed_update, at[c], tiles[c], count, sources, projection_t, global_embed, embed_momentum, groups,
            state["embed"],
        )

    def received(c, steps):
        return [x for n in range(steps) for x in (came[c][n], other[c][n])]

    project_send(0)
    l_away = swap_groups(run(widen, l_send, [sum(sizes)], local)[0], 1)
    project_keep(0)
    project_send(1)
    chip = run(widen, l_keep, sizes, local, l_away)
    layer_send(0)
    project_keep(1)
    far_send(0)
    layer_sum(0)
    far_sum(0)
    spread(0)
    far_send(1)
    finish(0, own, 2, whole_block[0])
    layer_finish(0)
    step(0, 0)
    far_sum(1)
    spread(1)
    finish(0, beside, 2, *received(0, 1))
    step(0, 1)
    step(1, 0)
    layer_send(1)
    finish(1, near, 4, whole_block[1], *received(1, 1))
    step(0, 2)
    step(1, 1)
    finish(0, far, 4, *received(0, 3))
    step(1, 2)
    layer_sum(1)
    finish(1, far, 4, *received(1, 3))
    layer_finish(1)
    new_layer, new_layer_momentum = (x.reshape(global_layer.shape) for x in state["layer"])
    return (new_layer, new_layer_momentum, *state["embed"])


def solution(mesh):
    in_specs = (
        P(None, "tensor", "shards"),
        P("groups", None, "tensor", "shards"),
        P(None, "tensor", "shards"),
        P("shards", "tensor"),
        P("groups", "shards", "tensor"),
        P("shards", "tensor"),
        P("tensor", None),
    )
    out_specs = (
        P(None, "tensor", "shards"),
        P(None, "tensor", "shards"),
        P("shards", "tensor"),
        P("shards", "tensor"),
    )
    return jax.shard_map(body, mesh=mesh, in_specs=in_specs, out_specs=out_specs, check_vma=False)
```

```python
import functools

import jax
import jax.numpy as jnp
import numpy as np
from jax import lax
from jax.experimental import pallas as pl
from jax.experimental.pallas import tpu as pltpu
from jax.sharding import PartitionSpec as P

momentum_rate = 0.9
outer_rate = 0.7
GRAIN = 16
UNIT = 176
COST = pl.CostEstimate(flops=0, bytes_accessed=0, transcendentals=0)
PARAMS = pltpu.CompilerParams(vmem_limit_bytes=53 * 1024 * 1024)


def nesterov(weights, momentum, delta):
    moved = momentum_rate * momentum + delta
    return (weights - outer_rate * (delta + momentum_rate * moved), moved)


def halves(value):
    high = value.astype(jnp.bfloat16)
    return high, (value - high.astype(jnp.float32)).astype(jnp.bfloat16)


def dot(a, b):
    return jnp.dot(a, b, preferred_element_type=jnp.float32)


class Table:
    def __init__(self, groups, tensor):
        self.shape = (groups, tensor)
        self.columns = []
        self.size = 0

    def add(self, entry):
        block = np.array([[entry(g, z) for z in range(self.shape[1])] for g in range(self.shape[0])], np.int32)
        at = self.size
        self.columns.append(block)
        self.size += block.shape[2]
        return at

    def mine(self):
        whole = jnp.asarray(np.concatenate(self.columns, axis=2))
        row = lax.dynamic_slice(
            whole, (lax.axis_index("groups"), lax.axis_index("tensor"), 0), (1, 1, self.size)
        )
        return row.reshape(self.size)


HBM = pl.BlockSpec(memory_space=pltpu.HBM)
VMEM = pl.BlockSpec(memory_space=pltpu.VMEM)
SMEM = pl.BlockSpec(memory_space=pltpu.SMEM)
ANY = pl.BlockSpec(memory_space=pl.ANY)


def rows_at(ref, place, unit, offset, size):
    return ref.at[pl.ds(pl.multiple_of(place * unit + offset, 8), size)]


def project_kernel(at, count, tile, tab, g, l, p, *refs):
    out, g_in, l_in, p_in, w, sem, p_sem = refs[-7:]
    rank, width = p.shape
    half = tile // 2
    fetch = pltpu.make_async_copy(p, p_in, p_sem)
    fetch.start()
    copies = []
    for i in range(count):
        pair = [
            pltpu.make_async_copy(rows_at(x, tab[at + i], GRAIN, 0, tile), to.at[i], sem.at[n, i])
            for n, (x, to) in enumerate(((g, g_in), (l, l_in)))
        ]
        for copy in pair:
            copy.start()
        copies.append(pair)
    fetch.wait()
    high, low = (x.T for x in halves(p_in[...]))
    none = jnp.zeros_like(high)
    w[0:width] = jnp.concatenate([high, none, low, none], axis=1)
    w[width:] = jnp.concatenate([none, high, none, low], axis=1)
    for i in range(count):
        for copy in copies[i]:
            copy.wait()
        difference = g_in[i] - l_in[i].astype(jnp.float32)
        high, low = halves(jnp.concatenate([difference[:half], difference[half:]], axis=1))
        wide = dot(high, w[...])
        mine = wide[:, 0 : 2 * rank] + wide[:, 2 * rank :] + dot(low, w[:, 0 : 2 * rank])
        rows = slice(i * half, (i + 1) * half)
        out[rows] = mine + refs[0][rows] if len(refs) > 7 else mine


def project(tab, at, count, tile, global_embed, local_embed, projection_t, *got):
    width = global_embed.shape[1]
    rank = projection_t.shape[0]
    return pl.pallas_call(
        functools.partial(project_kernel, at, count, tile),
        in_specs=[SMEM, HBM, HBM, HBM] + [VMEM] * len(got),
        out_specs=VMEM,
        out_shape=jax.ShapeDtypeStruct((count * tile // 2, 2 * rank), jnp.float32),
        scratch_shapes=[
            pltpu.VMEM((count, tile, width), jnp.float32),
            pltpu.VMEM((count, tile, width), jnp.bfloat16),
            pltpu.VMEM((rank, width), jnp.float32),
            pltpu.VMEM((2 * width, 4 * rank), jnp.bfloat16),
            pltpu.SemaphoreType.DMA((2, count)),
            pltpu.SemaphoreType.DMA(()),
        ],
        compiler_params=PARAMS,
        cost_estimate=COST,
        name="project",
    )(tab, global_embed, local_embed, projection_t, *got)


def update_kernel(at, unit, sub, subs, depth, parts, delta_of, extra, fixed, scratch, tab, *refs):
    far, (g, m) = refs[:extra], refs[extra : extra + 2]
    refs, scratch = refs[: len(refs) - scratch - fixed], refs[len(refs) - scratch - fixed :]
    new_g, new_m, g_in, m_in, g_out, m_out, packed, sem, source_sem, constant_sem = refs[-10:]
    near, scratch = scratch[:fixed], scratch[fixed:]
    count = parts

    def incoming(i, j):
        place, n = tab[at + count + i], i * subs + j
        return [
            pltpu.make_async_copy(rows_at(x, place, unit, j * sub, sub), to.at[n], sem.at[k, n])
            for k, (x, to) in enumerate(((g, g_in), (m, m_in)))
        ]

    def outgoing(i, j):
        place, n = tab[at + count + i], i * subs + j
        return [
            pltpu.make_async_copy(x.at[n], rows_at(to, place, unit, j * sub, sub), sem.at[2 + k, n])
            for k, (x, to) in enumerate(((g_out, new_g), (m_out, new_m)))
        ]

    def when_there(i, step):
        pl.when(tab[at + i] == 1)(step)

    def brought(i, source):
        here = pl.ds(pl.multiple_of(tab[at + 3 * count + i] * depth, 8), depth)
        return pltpu.make_async_copy(far[source].at[here], packed.at[i], source_sem.at[i])

    constant = [pltpu.make_async_copy(x, to, constant_sem) for x, to in zip(far[extra - fixed :], near)]
    for copy in constant:
        copy.start()
    for i in range(count):

        @functools.partial(when_there, i)
        def _(i=i):
            for n in range(extra - fixed):

                @pl.when(tab[at + 2 * count + i] == n)
                def _(n=n):
                    brought(i, n).start()

            for j in range(subs):
                for copy in incoming(i, j):
                    copy.start()

    for copy in constant:
        copy.wait()
    delta = delta_of(scratch, near)
    for i in range(count):

        @functools.partial(when_there, i)
        def _(i=i):
            brought(i, 0).wait()
            change = delta(packed.at[i])
            for j in range(subs):
                n = i * subs + j
                for copy in incoming(i, j):
                    copy.wait()
                weights = g_in[n]
                g_out[n], m_out[n] = nesterov(weights, m_in[n], change(j, weights))
                for copy in outgoing(i, j):
                    copy.start()

    for i in range(count):

        @functools.partial(when_there, i)
        def _(i=i):
            for j in range(subs):
                for copy in outgoing(i, j):
                    copy.wait()


def update(
    tab, at, unit, sub, subs, depth, parts, delta_of, sources, constants, weights, momentum, before, scratch, name
):
    rows, width = weights.shape
    extra = [] if before is None else list(before)
    count = parts * subs
    inputs = [*sources, *constants]
    where = 3 + len(inputs)
    return pl.pallas_call(
        functools.partial(
            update_kernel, at, unit, sub, subs, depth, parts, delta_of, len(inputs), len(constants), len(scratch)
        ),
        in_specs=[SMEM] + [ANY] * len(inputs) + [HBM] * (2 + len(extra)),
        out_specs=[HBM, HBM],
        out_shape=[jax.ShapeDtypeStruct((rows, width), jnp.float32)] * 2,
        input_output_aliases={} if before is None else {where: 0, where + 1: 1},
        scratch_shapes=[pltpu.VMEM((count, sub, width), jnp.float32)] * 4
        + [pltpu.VMEM((parts, depth, sources[0].shape[1]), jnp.float32)]
        + [pltpu.SemaphoreType.DMA((4, count)), pltpu.SemaphoreType.DMA((parts,)), pltpu.SemaphoreType.DMA(())]
        + [pltpu.VMEM(x.shape, x.dtype) for x in constants]
        + scratch,
        compiler_params=PARAMS,
        cost_estimate=COST,
        name=name,
    )(tab, *inputs, weights, momentum, *extra)


def embed_update(tab, at, tile, parts, sources, projection_t, weights, momentum, groups, before):
    width = weights.shape[1]
    rank = projection_t.shape[0]
    half = tile // 2

    def delta_of(scratch, refs):
        (w,) = scratch
        high, low = halves(refs[0][...])
        w[...] = jnp.zeros_like(w)
        for j in range(2):
            w[j, j * rank : (j + 1) * rank] = high
            w[j, (2 + j) * rank : (3 + j) * rank] = high
            w[j, (4 + j) * rank : (5 + j) * rank] = low

        def delta(packed):
            high, low = halves(packed[...] * (1 / groups))
            parts = jnp.concatenate([high, low, high], axis=1)
            return lambda j, weights: dot(parts, w[j])

        return delta

    scratch = [pltpu.VMEM((2, 6 * rank, width), jnp.bfloat16)]
    return update(
        tab, at, GRAIN, half, 2, half, parts, delta_of, sources, [projection_t], weights, momentum, before, scratch,
        "embed_update",
    )


def layer_update(tab, at, parts, sources, weights, momentum, groups, before):
    def delta_of(scratch, refs):
        return lambda packed: lambda j, weights: weights - packed[...] * (1 / groups)

    return update(
        tab, at, UNIT, UNIT, 1, UNIT, parts, delta_of, sources, [], weights, momentum, before, [], "layer_update"
    )


def widen_kernel(at, sizes, tab, l, *refs):
    *got, l_in, sem = refs
    got, outs = got[: len(got) - len(sizes)], got[len(got) - len(sizes) :]
    copy = pltpu.make_async_copy(rows_at(l, tab[at], UNIT, 0, sum(sizes)), l_in, sem)
    copy.start()
    copy.wait()
    first = 0
    for out, size in zip(outs, sizes):
        value = l_in[first : first + size].astype(jnp.float32)
        out[...] = value + got[0][first : first + size] if got else value
        first += size


def widen(tab, at, sizes, local, *got):
    width = local.shape[1]
    return pl.pallas_call(
        functools.partial(widen_kernel, at, sizes),
        in_specs=[SMEM, HBM] + [VMEM] * len(got),
        out_specs=[VMEM] * len(sizes),
        out_shape=[jax.ShapeDtypeStruct((size, width), jnp.float32) for size in sizes],
        scratch_shapes=[pltpu.VMEM((sum(sizes), width), jnp.bfloat16), pltpu.SemaphoreType.DMA(())],
        compiler_params=PARAMS,
        cost_estimate=COST,
        name="widen",
    )(tab, local, *got)


class Order:
    def __init__(self):
        self.last = None

    def after(self, x):
        if self.last is None:
            return x
        return lax.optimization_barrier((x, self.last))[0]

    def done(self, x):
        self.last = x[0] if isinstance(x, (list, tuple)) else x
        return x


def swap_groups(x, bit):
    return lax.ppermute(x, "groups", [(g, g ^ bit) for g in range(4)])


def shift(x, step):
    pairs = []
    for g in range(4):
        for z in range(4):
            to = z + 1 if g % 2 == 0 else z - 1
            first = z if g % 2 == 0 else 3 - z
            if 0 <= to < 4 and first >= step:
                pairs.append((g * 4 + z, g * 4 + to))
    return lax.ppermute(x, ("groups", "tensor"), pairs)


def plain(
    global_layer, local_layer, layer_momentum, global_embed, local_embed, embed_momentum, projection
):
    groups = lax.axis_size("groups")
    exact = {"precision": lax.Precision.HIGHEST, "preferred_element_type": jnp.float32}
    projected = jnp.dot(global_embed - local_embed[0].astype(jnp.float32), projection, **exact)
    projected = lax.psum(projected, ("groups", "tensor")) / groups
    layer_delta = lax.psum(global_layer - local_layer[0].astype(jnp.float32), "groups") / groups
    embed_delta = jnp.dot(projected, projection.T, **exact)
    return (
        *nesterov(global_layer, layer_momentum, layer_delta),
        *nesterov(global_embed, embed_momentum, embed_delta),
    )


def body(
    global_layer, local_layer, layer_momentum, global_embed, local_embed, embed_momentum, projection
):
    groups = lax.axis_size("groups")
    tensor = lax.axis_size("tensor")
    rows, width = global_embed.shape
    weights = global_layer.reshape(-1, global_layer.shape[-1])
    units = weights.shape[0] // UNIT // 2
    grains = rows // (8 * GRAIN)
    whole = rows % (8 * GRAIN) == 0 and 8 <= grains <= 125 and weights.shape[0] % (2 * UNIT) == 0 and units == 6
    if not whole or (groups, tensor) != (4, 4) or width % 256 or projection.shape[1] != 64:
        return plain(
            global_layer, local_layer, layer_momentum, global_embed, local_embed, embed_momentum, projection
        )
    projection_t = projection.T
    embed_local = local_embed[0]
    momentum = layer_momentum.reshape(weights.shape)
    local = local_layer[0].reshape(weights.shape)
    table = Table(groups, tensor)
    chunks = [grains * 14 // 25]
    chunks.append(grains - sum(chunks))
    tiles = [n * GRAIN for n in chunks]
    bases = [0, 8 * chunks[0]]

    def core(g):
        return g % 2

    def place(c, h, k):
        return bases[c] + (h * 4 + k) * chunks[c]

    p_send = [table.add(lambda g, z, c=c: [place(c, 1 - core(g), k) for k in range(4)]) for c in range(2)]
    p_keep = [table.add(lambda g, z, c=c: [place(c, core(g), k) for k in range(4)]) for c in range(2)]

    def blocks_at(c, turn):
        def entry(g, z):
            blocks = []
            for n in range(4):
                for h, k in ((core(g), z - n), (1 - core(g), z + n)):
                    k = 2 * z - k if core(g) else k
                    if n or h == core(g):
                        blocks.append((len(blocks), h, k))
            there = [b for b in blocks if 0 <= b[2] < 4]
            taken = (there[:1], there[1:2], there[2:], there[:2])[turn]
            parts = [(place(c, h ^ half, k), n - (turn in (1, 2)), half) for n, h, k in taken for half in (0, 1)]
            return [1] * len(parts) + [p for column in zip(*parts) for p in column]

        return table.add(entry)

    own, beside, far, near = ([blocks_at(c, turn) for c in range(2)] for turn in range(4))
    pieces = [3, 3]
    firsts = [sum(pieces[:n]) for n in range(len(pieces))]
    l_send = table.add(lambda g, z: [(1 - core(g)) * units])
    l_keep = table.add(lambda g, z: [core(g) * units])


    def l_place(n):
        def entry(g, z):
            parts = [
                ((core(g) ^ h) * units + firsts[n] + u, h, u) for h in (0, 1) for u in range(pieces[n])
            ]
            return [1] * len(parts) + [p for column in zip(*parts) for p in column]

        return table.add(entry)

    l_place_of = [l_place(n) for n in range(len(pieces))]
    tab = table.mine()
    order = Order()

    def run(kernel, at, *args):
        return order.done(kernel(order.after(tab), at, *args))

    def add(a, b):
        return order.done(order.after(a) + b)

    def wait(x):
        return order.done(order.after(x))

    embed = (global_embed, embed_local, projection_t)
    state = {"embed": None, "layer": None}
    sizes = [n * UNIT for n in pieces]
    l_got, l_total, l_other = ([None] * len(pieces) for _ in range(3))
    sent, kept, summed, whole_block = ([None] * 2 for _ in range(4))
    came = [[None] * 3, [None] * 3]
    other = [[None] * 3, [None] * 3]

    def layer_send(n):
        l_got[n] = swap_groups(order.after(chip[n]), 2)

    def layer_sum(n):
        l_total[n] = add(chip[n], l_got[n])
        l_other[n] = swap_groups(l_total[n], 1)

    def layer_finish(n):
        sources = (l_total[n], l_other[n])
        state["layer"] = run(
            layer_update, l_place_of[n], 2 * pieces[n], sources, weights, momentum, groups, state["layer"]
        )

    def project_send(c):
        sent[c] = swap_groups(run(project, p_send[c], 4, tiles[c], *embed), 1)

    def project_keep(c):
        chip = run(project, p_keep[c], 4, tiles[c], *embed, sent[c])
        chip = chip.reshape((4, -1) + chip.shape[1:])
        kept[c] = lax.all_to_all(chip, "tensor", 0, 0)

    def far_send(c):
        kept[c] = wait(kept[c])
        kept[c] = order.done((kept[c][0] + kept[c][1]) + (kept[c][2] + kept[c][3]))
        kept[c] = kept[c].reshape(-1, kept[c].shape[-1])
        summed[c] = swap_groups(kept[c], 2)

    def far_sum(c):
        summed[c] = add(kept[c], summed[c])
        whole_block[c] = swap_groups(summed[c], 1)

    def spread(c):
        whole_block[c] = order.done(jnp.concatenate([order.after(summed[c]), whole_block[c]]))
        came[c][0] = shift(whole_block[c], 0)

    def step(c, n):
        came[c][n] = wait(came[c][n])
        if n < 2:
            came[c][n + 1] = shift(came[c][n], n + 1)
        other[c][n] = swap_groups(came[c][n], 1)

    def finish(c, at, count, *sources):
        state["embed"] = run(
            embed_update, at[c], tiles[c], count, sources, projection_t, global_embed, embed_momentum, groups,
            state["embed"],
        )

    def received(c, steps):
        return [x for n in range(steps) for x in (came[c][n], other[c][n])]

    project_send(0)
    l_away = swap_groups(run(widen, l_send, [sum(sizes)], local)[0], 1)
    project_keep(0)
    project_send(1)
    chip = run(widen, l_keep, sizes, local, l_away)
    layer_send(0)
    project_keep(1)
    far_send(0)
    layer_sum(0)
    far_sum(0)
    spread(0)
    finish(0, own, 2, whole_block[0])
    far_send(1)
    layer_finish(0)
    step(0, 0)
    far_sum(1)
    spread(1)
    finish(0, beside, 2, *received(0, 1))
    step(0, 1)
    step(1, 0)
    layer_send(1)
    finish(1, near, 4, whole_block[1], *received(1, 1))
    step(0, 2)
    step(1, 1)
    finish(0, far, 4, *received(0, 3))
    step(1, 2)
    layer_sum(1)
    finish(1, far, 4, *received(1, 3))
    layer_finish(1)
    new_layer, new_layer_momentum = (x.reshape(global_layer.shape) for x in state["layer"])
    return (new_layer, new_layer_momentum, *state["embed"])


def solution(mesh):
    in_specs = (
        P(None, "tensor", "shards"),
        P("groups", None, "tensor", "shards"),
        P(None, "tensor", "shards"),
        P("shards", "tensor"),
        P("groups", "shards", "tensor"),
        P("shards", "tensor"),
        P("tensor", None),
    )
    out_specs = (
        P(None, "tensor", "shards"),
        P(None, "tensor", "shards"),
        P("shards", "tensor"),
        P("shards", "tensor"),
    )
    return jax.shard_map(body, mesh=mesh, in_specs=in_specs, out_specs=out_specs, check_vma=False)
```
